32 devices in a mesh: depth: 2 (over y), tile: 4 (over z), brick: 4 (over x, core).
Axes of the slice: x: 2, y: 2, z: 4, core: 2. Of those that a mesh axis runs over, the one named last changes fastest.
Arguments:
- fragments: float32 [2, 16, 16, 2, 16, 128], P('depth', ('tile', 'brick')), may hold values from 0 to 0.61, as said below
- layer_rank: int32 [2, 16, 16, 2, 4, 128], P('depth', ('tile', 'brick')), may hold values from 0 to 3, as said below
- pixel_count: int32 [2, 16, 16, 2], P('depth', ('tile', 'brick')), may hold values from 1 to 128
- slot_count: int32 [2, 16, 16], P('depth', ('tile', 'brick')), may hold values from 0 to 2, as said below
- block_run: int32 [2, 16, 16, 2], P('depth', ('tile', 'brick')), may hold values from 0 to 255, as said below
- brick_order: int32 [2, 16], P('depth'), may hold values from 0 to 15, each once within a row
- interlace: int32 [256], replicated, may hold values from 0 to 255, as said below
Outputs:
- image: float32 [16, 2, 128, 4, 128], P(('tile', 'brick'), 'depth')
The draws below stay inside these ranges and needn't reach their ends.
Inputs may be any that keep to these rules, and one draw needn't show every extreme that they name: `fragments`: each entry is r, g, b, alpha with alpha at least 0.003 and each color between 0 and alpha. `layer_rank`: at every pixel the four ranks are 0, 1, 2 and 3 in some order. `slot_count`: in every slab some owner receives 2 live blocks from every brick. `block_run`: the slots that one brick sends to one owner name distinct strip slots. `brick_order`: each slab's ranks name every brick once. `interlace`: each value once; every aligned group of 128 consecutive entries holds exactly 64 values of each aligned range of 128 values.
All inputs are finite; a program needn't handle non-finite values.
Results may differ from the reference program's by a relative error of at most 0.0003.
Values sent between devices are 32-bit elements; how exact they have to be, the bound alone decides.
A program may use at most 64 MiB of HBM per device.

```python
import math
import jax
import jax.numpy as jnp
from jax import lax

PIX = 128
CAP = 2
RUNS = 256
SLABS = 2
OWNERS = 16
Q = 128


def draw_fragments(key, part):
    alpha_key, color_key = jax.random.split(key)
    alpha_shape = (SLABS, OWNERS, OWNERS, CAP, 4, 1, PIX)
    color_shape = (SLABS, OWNERS, OWNERS, CAP, 4, 3, PIX)
    alpha = jnp.exp(jax.random.uniform(alpha_key, alpha_shape, jnp.float32, math.log(0.003), math.log(0.6)))
    color = alpha * jax.random.uniform(color_key, color_shape, jnp.float32)
    return jnp.concatenate([color, alpha], axis=5).reshape(SLABS, OWNERS, OWNERS, CAP, 16, PIX)


def draw_layer_rank(key, part):
    shape = (SLABS, OWNERS, OWNERS, CAP, 4, PIX)
    scores = jax.random.randint(key, shape, 0, 1 << 20) * 4 + lax.broadcasted_iota(jnp.int32, shape, 4)
    order = jnp.argsort(scores, axis=4)
    return jnp.argsort(order, axis=4).astype(jnp.int32)


def draw_slot_count(key, part):
    base_key, busy_key = jax.random.split(key)
    base = jax.random.randint(base_key, (SLABS, OWNERS, OWNERS), 0, CAP + 1)
    busy = jax.random.randint(busy_key, (SLABS,), 0, OWNERS)
    full = lax.broadcasted_iota(jnp.int32, (SLABS, OWNERS, OWNERS), 1) == busy[:, None, None]
    return jnp.where(full, CAP, base).astype(jnp.int32)


def draw_block_run(key, part):
    shape = (SLABS, OWNERS, OWNERS, RUNS)
    scores = jax.random.randint(key, shape, 0, 1 << 20) * RUNS + lax.broadcasted_iota(jnp.int32, shape, 3)
    return lax.top_k(scores, CAP)[1].astype(jnp.int32)


def draw_interlace(key, part):
    spread_key, shuffle_key = jax.random.split(key)
    per_tile = Q // SLABS
    tile_keys = jax.random.split(spread_key, SLABS)
    within = jax.vmap(lambda single: jax.random.permutation(single, Q))(tile_keys)
    base = lax.broadcasted_iota(jnp.int32, (SLABS, Q), 0) * Q
    screen = (within + base).reshape(SLABS, SLABS, per_tile)
    grouped = jnp.transpose(screen, (1, 0, 2)).reshape(SLABS, Q)
    piece_keys = jax.random.split(shuffle_key, SLABS)
    mixed = jax.vmap(lambda single, entries: jax.random.permutation(single, entries))(piece_keys, grouped)
    return mixed.reshape(RUNS).astype(jnp.int32)


def set_ends(drawn, rng, smallest, top_value):
    longest = drawn.shape.index(max(drawn.shape))
    spots = []
    for shift in (0, 1):
        where = [jax.random.randint(jax.random.fold_in(rng, axis), (), 0, length) for axis, length in enumerate(drawn.shape)]
        where[longest] = (where[longest] + shift) % drawn.shape[longest]
        spots.append(tuple(where))
    return drawn.at[spots[0]].set(smallest).at[spots[1]].set(top_value)


def setup_inputs(seed: int = 0) -> dict:
    keys = jax.random.split(jax.random.key(seed), 8)
    return {
        "fragments": draw_fragments(jax.random.fold_in(keys[7], 71), 0),
        "layer_rank": draw_layer_rank(jax.random.fold_in(keys[7], 71), 0),
        "pixel_count": set_ends(jax.random.randint(keys[2], (SLABS, OWNERS, OWNERS, CAP), 1, PIX + 1), jax.random.fold_in(keys[2], 1), 1, PIX).astype(jnp.int32),
        "slot_count": draw_slot_count(jax.random.fold_in(keys[7], 71), 0),
        "block_run": draw_block_run(jax.random.fold_in(keys[7], 71), 0),
        "brick_order": jax.vmap(lambda own: jax.random.permutation(own, OWNERS))(jax.random.split(keys[5], SLABS)).reshape((SLABS, OWNERS)).astype(jnp.int32),
        "interlace": draw_interlace(jax.random.fold_in(keys[7], 71), 0),
    }


def order_layers(layers, ranks, counts):
    width = layers.shape[-1]
    pixel = lax.broadcasted_iota(jnp.int32, counts.shape + (width,), 2)
    visible = (pixel < counts[:, :, None]).astype(jnp.float32)
    placed = []
    for position in range(4):
        chosen = jnp.zeros(layers.shape[:2] + layers.shape[3:], jnp.float32)
        for layer in range(4):
            picked = (ranks[:, :, layer, :] == position).astype(jnp.float32)
            chosen = chosen + picked[:, :, None, :] * layers[:, :, layer]
        placed.append(chosen * visible[:, :, None, :])
    return jnp.stack(placed, axis=2)


def blend(layers):
    result = layers[..., 3, :, :]
    for position in (2, 1, 0):
        front = layers[..., position, :, :]
        result = front + (1.0 - front[..., 3:4, :]) * result
    return result


def over(front, back):
    return front + (1.0 - front[..., 3:4, :]) * back


def compose_strip(blocks, live, runs, brick_rank, slots):
    keeping = jnp.log(1.0 - blocks[:, 3, :] * live[:, None])
    same = runs[:, None] == runs[None, :]
    before = brick_rank[None, :] < brick_rank[:, None]
    earlier = (same & before).astype(jnp.float32)
    passed = jnp.exp(jnp.dot(earlier, keeping, precision=lax.Precision.HIGHEST))
    shaded = (blocks * live[:, None, None] * passed[:, None, :]).reshape(blocks.shape[0], 4 * blocks.shape[-1])
    target = (lax.broadcasted_iota(jnp.int32, (slots, runs.shape[0]), 0) == runs[None, :]).astype(jnp.float32)
    strip = jnp.dot(target, shaded, precision=lax.Precision.HIGHEST)
    return strip.reshape(slots, 4, blocks.shape[-1])


def slab_image(pieces):
    fragments, layer_rank, pixel_count, slot_count, block_run, brick_order = pieces
    owners = fragments.shape[0]
    capacity = fragments.shape[2]
    width = fragments.shape[-1]
    layers = fragments.reshape(owners * owners, capacity, 4, 4, width)
    ordered = order_layers(layers, layer_rank.reshape(owners * owners, capacity, 4, width), pixel_count.reshape(owners * owners, capacity))
    blocks = blend(ordered).reshape(owners, owners, capacity, 4, width)

    def one_owner(target):
        incoming = lax.dynamic_index_in_dim(blocks, target, 1, keepdims=False).reshape(owners * capacity, 4, width)
        counts = lax.dynamic_index_in_dim(slot_count, target, 0, keepdims=False)
        runs = lax.dynamic_index_in_dim(block_run, target, 0, keepdims=False).reshape(owners * capacity)
        live = (lax.broadcasted_iota(jnp.int32, (owners, capacity), 1) < counts[:, None]).astype(jnp.float32).reshape(owners * capacity)
        brick_rank = jnp.repeat(brick_order, capacity)
        return compose_strip(incoming, live, runs, brick_rank, RUNS)

    return lax.map(one_owner, jnp.arange(owners, dtype=jnp.int32))


def reference(fragments, layer_rank, pixel_count, slot_count, block_run, brick_order, interlace):
    strips = lax.map(slab_image, (fragments, layer_rank, pixel_count, slot_count, block_run, brick_order))
    total = strips[0]
    for slab in range(1, SLABS):
        total = over(total, strips[slab])
    image = jnp.zeros_like(total).at[:, interlace].set(total)
    return image.reshape(OWNERS, SLABS, Q, 4, PIX)
```

```python
import functools

import jax
import jax.numpy as jnp
from jax import lax
from jax.experimental import pallas as pl
from jax.experimental.pallas import tpu as pltpu
from jax.sharding import PartitionSpec as P

MESH = pl.DeviceIdType.MESH
F32 = jnp.float32
BF16 = jnp.bfloat16


def iota(shape, dim):
    return lax.broadcasted_iota(jnp.int32, shape, dim)


def log2(n):
    assert n & (n - 1) == 0
    return n.bit_length() - 1


def each(count, body):
    if count <= 32:
        for i in range(count):
            body(i)
    else:
        lax.fori_loop(0, count, lambda i, c: (body(i), c)[1], 0)


def column(row, rows):
    shape = (rows, row.shape[1])
    return jnp.sum(jnp.where(iota(shape, 0) == iota(shape, 1), row, 0.0), axis=1, keepdims=True)


def split(x):
    high = x.astype(BF16)
    low = (x - high.astype(F32)).astype(BF16)
    return jnp.concatenate([high, low], axis=0)


def blend(frag, rank, count, send, owners, capacity):
    pixel = iota((owners, frag.shape[-1]), 1).astype(F32)
    limit = count[...].astype(F32)
    for slot in range(capacity):
        ranks = [rank[pl.ds(slot * 4 + l, owners, stride=capacity * 4), :] for l in range(4)]
        value = [
            [frag[pl.ds(slot * 16 + l * 4 + e, owners, stride=capacity * 16), :] for e in range(4)]
            for l in range(4)
        ]
        clear = [1.0 - value[l][3] for l in range(4)]
        through = [None] * 4
        for l in range(4):
            for m in range(l):
                front = ranks[m] < ranks[l]
                behind = jnp.where(front, clear[m], 1.0)
                ahead = jnp.where(front, 1.0, clear[l])
                through[l] = behind if through[l] is None else through[l] * behind
                through[m] = ahead if through[m] is None else through[m] * ahead
        visible = pixel < column(limit[slot : slot + 1, :], owners)
        for e in range(4):
            total = value[0][e] * through[0]
            for l in range(1, 4):
                total = total + value[l][e] * through[l]
            send[pl.ds(slot * 4 + e, owners, stride=capacity * 4), :] = jnp.where(visible, total, 0.0)


def describe(slots, runs, order, place, blocks, owners, capacity, meta):
    width = meta.shape[1]
    lane = iota((owners, width), 1) & (blocks - 1)
    own = (lane >> log2(owners * capacity)) == place
    brick = (lane >> log2(capacity)) & (owners - 1)
    slot = lane & (capacity - 1)
    chosen = own & (brick == iota((owners, width), 0))
    live = slot.astype(F32) < column(slots.astype(F32), owners)
    runs = runs.astype(F32)
    run = jnp.broadcast_to(column(runs[0:1, :], owners), (owners, width))
    for c in range(1, capacity):
        run = jnp.where(slot == c, column(runs[c : c + 1, :], owners), run)
    key = jnp.sum(jnp.where(chosen & live, run + 1.0, 0.0), axis=0, keepdims=True)
    depth = column(order.astype(F32), owners) + (place * owners).astype(F32)
    rank = jnp.sum(jnp.where(chosen, depth, 0.0), axis=0, keepdims=True)
    row = iota(meta.shape, 0)
    meta[...] = jnp.where(row == 0, key, jnp.where(row == 1, rank, 0.0))


def exchange(sizes, frag_hbm, rank_hbm, count_hbm, slots_hbm, runs_hbm, order_hbm, lace_hbm,
             recv, earlier, target,
             frag, rank, count, slots, runs, order, lace, send, meta,
             load_sem, send_sem, recv_sem, meta_send, meta_recv):
    depths, tiles, bricks, owners, capacity, share = sizes
    d, t, b = lax.axis_index("depth"), lax.axis_index("tile"), lax.axis_index("brick")
    blocks = depths * owners * capacity
    group = capacity * 4
    others = depths * tiles * bricks - 1

    loads = [
        pltpu.make_async_copy(src, dst, load_sem.at[i])
        for i, (src, dst) in enumerate([
            (frag_hbm, frag), (rank_hbm, rank), (count_hbm, count), (slots_hbm, slots),
            (runs_hbm, runs), (order_hbm, order), (lace_hbm, lace),
        ])
    ]
    for load in loads:
        load.start()

    def device(k):
        k = k + 1
        kt = (k // (depths * bricks)) % tiles
        kd = (k // bricks) % depths
        kb = k % bricks
        return (d + kd) % depths, (t + kt) % tiles, (b + kb) % bricks

    barrier = pltpu.get_barrier_semaphore()

    def greet(k):
        pl.semaphore_signal(barrier, inc=1, device_id=device(k), device_id_type=MESH)

    each(others, greet)

    for load in loads[2:]:
        load.wait()
    describe(slots[...], runs[...], order[...], d, blocks, owners, capacity, meta.at[d])
    loads[0].wait()
    loads[1].wait()
    blend(frag, rank, count, send, owners, capacity)
    mine = t * bricks + b
    source = pl.ds(pl.multiple_of((d * owners + mine) * group, group), group)

    pl.semaphore_wait(barrier, others)

    def tell(k):
        pltpu.make_async_remote_copy(
            src_ref=meta.at[d], dst_ref=meta.at[d], send_sem=meta_send, recv_sem=meta_recv,
            device_id=((d + k + 1) % depths, t, b), device_id_type=MESH,
        ).start()

    if depths > 1:
        each(depths - 1, tell)

    def deliver(k):
        to = device(k)
        owner = to[1] * bricks + to[2]
        pltpu.make_async_remote_copy(
            src_ref=send.at[pl.ds(pl.multiple_of(owner * group, group), group)],
            dst_ref=recv.at[source], send_sem=send_sem, recv_sem=recv_sem,
            device_id=to, device_id_type=MESH,
        ).start()

    each(others, deliver)
    recv[source, :] = send[pl.ds(pl.multiple_of(mine * group, group), group), :]

    slots_total = lace.shape[0] * lace.shape[1]
    place = lace[...] - d * share
    shown = jnp.concatenate(
        [
            jnp.where(place[i : i + 1, :] == iota((share, lace.shape[1]), 0), 1.0, 0.0)
            for i in range(lace.shape[0])
        ],
        axis=1,
    ).astype(BF16)

    if depths > 1:
        part = meta.at[pl.ds(0, depths - 1)]
        pltpu.make_async_copy(part, part, meta_recv).wait()
    known = meta[0]
    for s in range(1, depths):
        known = known + meta[s]
    key, rank_row = known[0:1, :], known[1:2, :]
    same = column(key, blocks) == key
    before = rank_row < column(rank_row, blocks)
    earlier[...] = jnp.where(same & before, 1.0, 0.0).astype(BF16)
    holds = iota((slots_total, 2 * blocks), 0).astype(F32) + 1.0 == key
    target[...] = jnp.dot(
        shown, jnp.where(holds, 1.0, 0.0).astype(BF16), preferred_element_type=F32
    ).astype(BF16)

    whole = recv.at[pl.ds(0, others * group)]
    pltpu.make_async_copy(whole, whole, recv_sem).wait()
    pltpu.make_async_copy(whole, whole, send_sem).wait()
    if depths > 1:
        pltpu.make_async_copy(part, part, meta_send).wait()


def compose(recv, earlier, target, out):
    blocks = earlier.shape[0]
    share = target.shape[0]
    clear = jnp.log(1.0 - recv[pl.ds(3, blocks, stride=4), :])
    passed = jnp.exp(jnp.dot(earlier[...], split(clear), preferred_element_type=F32))
    for e in range(4):
        shaded = recv[pl.ds(e, blocks, stride=4), :] * passed
        out[pl.ds(e, share, stride=4), :] = jnp.dot(
            target[...], split(shaded), preferred_element_type=F32
        )


def shards(fragments, layer_rank, pixel_count, slot_count, block_run, brick_order, interlace):
    owners, capacity, width = fragments.shape[2], fragments.shape[3], fragments.shape[-1]
    runs_total = interlace.shape[0]
    depths, tiles, bricks = (lax.axis_size(a) for a in ("depth", "tile", "brick"))
    share = runs_total // depths
    blocks = depths * owners * capacity
    lanes = min(128, runs_total)
    args = [
        fragments.reshape(owners * capacity * 16, width),
        layer_rank.reshape(owners * capacity * 4, width),
        pixel_count.reshape(owners, capacity).T,
        slot_count.reshape(1, owners),
        block_run.reshape(owners, capacity).T,
        brick_order.reshape(1, owners),
        interlace.reshape(runs_total // lanes, lanes),
    ]
    vmem = pl.BlockSpec(memory_space=pltpu.VMEM)
    recv, earlier, target = pl.pallas_call(
        functools.partial(exchange, (depths, tiles, bricks, owners, capacity, share)),
        out_shape=(
            jax.ShapeDtypeStruct((blocks * 4, width), F32),
            jax.ShapeDtypeStruct((blocks, 2 * blocks), BF16),
            jax.ShapeDtypeStruct((share, 2 * blocks), BF16),
        ),
        in_specs=[pl.BlockSpec(memory_space=pl.ANY)] * len(args),
        out_specs=(vmem, vmem, vmem),
        scratch_shapes=[pltpu.VMEM(a.shape, a.dtype) for a in args]
        + [
            pltpu.VMEM((owners * capacity * 4, width), F32),
            pltpu.VMEM((depths, 8, 2 * blocks), F32),
            pltpu.SemaphoreType.DMA((len(args),)),
            pltpu.SemaphoreType.DMA,
            pltpu.SemaphoreType.DMA,
            pltpu.SemaphoreType.DMA,
            pltpu.SemaphoreType.DMA,
        ],
        compiler_params=pltpu.CompilerParams(
            collective_id=0, has_side_effects=True, vmem_limit_bytes=32 * 1024 * 1024
        ),
        name="exchange",
    )(*args)
    image = pl.pallas_call(
        compose,
        out_shape=jax.ShapeDtypeStruct((share * 4, width), F32),
        in_specs=[vmem] * 3,
        out_specs=vmem,
        compiler_params=pltpu.CompilerParams(vmem_limit_bytes=32 * 1024 * 1024),
        name="compose",
    )(recv, earlier, target)
    return image.reshape(1, 1, share, 4, width)


def solution(mesh):
    return jax.shard_map(
        shards,
        mesh=mesh,
        in_specs=(
            P("depth", ("tile", "brick"), None, None, None, None),
            P("depth", ("tile", "brick"), None, None, None, None),
            P("depth", ("tile", "brick"), None, None),
            P("depth", ("tile", "brick"), None),
            P("depth", ("tile", "brick"), None, None),
            P("depth", None),
            P(),
        ),
        out_specs=P(("tile", "brick"), "depth", None, None, None),
        check_vma=False,
    )
```

```python
import functools

import jax
import jax.numpy as jnp
from jax import lax
from jax.experimental import pallas as pl
from jax.experimental.pallas import tpu as pltpu
from jax.sharding import PartitionSpec as P

MESH = pl.DeviceIdType.MESH
F32 = jnp.float32
BF16 = jnp.bfloat16


def iota(shape, dim):
    return lax.broadcasted_iota(jnp.int32, shape, dim)


def log2(n):
    assert n & (n - 1) == 0
    return n.bit_length() - 1


def column(row, rows):
    shape = (rows, row.shape[1])
    return jnp.sum(jnp.where(iota(shape, 0) == iota(shape, 1), row, 0.0), axis=1, keepdims=True)


def split(x):
    high = x.astype(BF16)
    low = (x - high.astype(F32)).astype(BF16)
    return jnp.concatenate([high, low], axis=0)


def blend(frag, rank, count, send, owners, capacity):
    pixel = iota((owners, frag.shape[-1]), 1).astype(F32)
    limit = count[...].astype(F32)
    for slot in range(capacity):
        ranks = [rank[pl.ds(slot * 4 + l, owners, stride=capacity * 4), :] for l in range(4)]
        value = [
            [frag[pl.ds(slot * 16 + l * 4 + e, owners, stride=capacity * 16), :] for e in range(4)]
            for l in range(4)
        ]
        clear = [1.0 - value[l][3] for l in range(4)]
        through = [None] * 4
        for l in range(4):
            for m in range(l):
                front = ranks[m] < ranks[l]
                behind = jnp.where(front, clear[m], 1.0)
                ahead = jnp.where(front, 1.0, clear[l])
                through[l] = behind if through[l] is None else through[l] * behind
                through[m] = ahead if through[m] is None else through[m] * ahead
        visible = pixel < column(limit[slot : slot + 1, :], owners)
        for e in range(4):
            total = value[0][e] * through[0]
            for l in range(1, 4):
                total = total + value[l][e] * through[l]
            send[pl.ds(slot * 4 + e, owners, stride=capacity * 4), :] = jnp.where(visible, total, 0.0)


def describe(slots, runs, order, place, blocks, owners, capacity, meta):
    width = meta.shape[1]
    lane = iota((owners, width), 1) & (blocks - 1)
    own = (lane >> log2(owners * capacity)) == place
    brick = (lane >> log2(capacity)) & (owners - 1)
    slot = lane & (capacity - 1)
    chosen = own & (brick == iota((owners, width), 0))
    live = slot.astype(F32) < column(slots.astype(F32), owners)
    runs = runs.astype(F32)
    run = jnp.broadcast_to(column(runs[0:1, :], owners), (owners, width))
    for c in range(1, capacity):
        run = jnp.where(slot == c, column(runs[c : c + 1, :], owners), run)
    key = jnp.sum(jnp.where(chosen & live, run + 1.0, 0.0), axis=0, keepdims=True)
    depth = column(order.astype(F32), owners) + (place * owners).astype(F32)
    rank = jnp.sum(jnp.where(chosen, depth, 0.0), axis=0, keepdims=True)
    row = iota(meta.shape, 0)
    meta[...] = jnp.where(row == 0, key, jnp.where(row == 1, rank, 0.0))


def exchange(sizes, frag_hbm, rank_hbm, count_hbm, slots_hbm, runs_hbm, order_hbm, lace_hbm,
             recv, earlier, target,
             frag, rank, count, slots, runs, order, lace, send, meta,
             load_sem, send_sem, recv_sem, pass_send, pass_recv, meta_send, meta_recv):
    depths, tiles, bricks, owners, capacity, share = sizes
    d, t, b = lax.axis_index("depth"), lax.axis_index("tile"), lax.axis_index("brick")
    blocks = depths * owners * capacity
    group = capacity * 4

    loads = [
        pltpu.make_async_copy(src, dst, load_sem.at[i])
        for i, (src, dst) in enumerate([
            (frag_hbm, frag), (rank_hbm, rank), (count_hbm, count), (slots_hbm, slots),
            (runs_hbm, runs), (order_hbm, order), (lace_hbm, lace),
        ])
    ]
    for load in loads:
        load.start()

    def away(own, k):
        for bit in range(k.bit_length()):
            if k >> bit & 1:
                own = own + (1 - 2 * ((own // (1 << bit)) % 2)) * (1 << bit)
        return own

    half = tiles // 2
    far = list(range(half, tiles)) + list(range(half - 1, -1, -1))
    mates = [(d, away(t, kt), away(b, kb)) for kt in far for kb in range(bricks) if kt or kb]
    partners = [(away(d, kd), t, b) for kd in range(1, depths)]
    barrier = pltpu.get_barrier_semaphore()
    for to in mates + partners:
        pl.semaphore_signal(barrier, inc=1, device_id=to, device_id_type=MESH)

    for load in loads[2:]:
        load.wait()
    describe(slots[...], runs[...], order[...], d, blocks, owners, capacity, meta.at[d])
    loads[0].wait()
    loads[1].wait()
    blend(frag, rank, count, send, owners, capacity)
    mine = t * bricks + b
    source = pl.ds(pl.multiple_of((d * owners + mine) * group, group), group)

    pl.semaphore_wait(barrier, len(mates) + len(partners))

    for to in partners:
        pltpu.make_async_remote_copy(
            src_ref=meta.at[d], dst_ref=meta.at[d], send_sem=meta_send, recv_sem=meta_recv,
            device_id=to, device_id_type=MESH,
        ).start()
    for to in mates:
        owner = to[1] * bricks + to[2]
        pltpu.make_async_remote_copy(
            src_ref=send.at[pl.ds(pl.multiple_of(owner * group, group), group)],
            dst_ref=recv.at[source], send_sem=send_sem, recv_sem=recv_sem.at[t],
            device_id=to, device_id_type=MESH,
        ).start()
    recv[source, :] = send[pl.ds(pl.multiple_of(mine * group, group), group), :]

    slots_total = lace.shape[0] * lace.shape[1]
    place = lace[...] - d * share
    shown = jnp.concatenate(
        [
            jnp.where(place[i : i + 1, :] == iota((share, lace.shape[1]), 0), 1.0, 0.0)
            for i in range(lace.shape[0])
        ],
        axis=1,
    ).astype(BF16)

    near = ([1, 0] if tiles > 1 else [0]) + list(range(tiles - 1, 1, -1))
    for kt in near:
        tile = away(t, kt)
        count_in = bricks if kt else bricks - 1
        if count_in:
            bytes_in = recv.at[pl.ds(0, count_in * group)]
            pltpu.make_async_copy(bytes_in, bytes_in, recv_sem.at[tile]).wait()
        rows = pl.ds(
            pl.multiple_of((d * owners + tile * bricks) * group, group * bricks), group * bricks
        )
        for to in partners:
            pltpu.make_async_remote_copy(
                src_ref=recv.at[rows], dst_ref=recv.at[rows], send_sem=pass_send, recv_sem=pass_recv,
                device_id=to, device_id_type=MESH,
            ).start()

    if partners:
        part = meta.at[pl.ds(0, depths - 1)]
        pltpu.make_async_copy(part, part, meta_recv).wait()
    known = meta[0]
    for s in range(1, depths):
        known = known + meta[s]
    key, rank_row = known[0:1, :], known[1:2, :]
    same = column(key, blocks) == key
    before = rank_row < column(rank_row, blocks)
    earlier[...] = jnp.where(same & before, 1.0, 0.0).astype(BF16)
    holds = iota((slots_total, 2 * blocks), 0).astype(F32) + 1.0 == key
    target[...] = jnp.dot(
        shown, jnp.where(holds, 1.0, 0.0).astype(BF16), preferred_element_type=F32
    ).astype(BF16)

    if partners:
        passed = recv.at[pl.ds(0, (depths - 1) * owners * group)]
        pltpu.make_async_copy(passed, passed, pass_recv).wait()
        pltpu.make_async_copy(passed, passed, pass_send).wait()
        pltpu.make_async_copy(part, part, meta_send).wait()
    if mates:
        sent = recv.at[pl.ds(0, len(mates) * group)]
        pltpu.make_async_copy(sent, sent, send_sem).wait()


def compose(recv, earlier, target, out):
    blocks = earlier.shape[0]
    share = target.shape[0]
    clear = jnp.log(1.0 - recv[pl.ds(3, blocks, stride=4), :])
    passed = jnp.exp(jnp.dot(earlier[...], split(clear), preferred_element_type=F32))
    for e in range(4):
        shaded = recv[pl.ds(e, blocks, stride=4), :] * passed
        out[pl.ds(e, share, stride=4), :] = jnp.dot(
            target[...], split(shaded), preferred_element_type=F32
        )


def shards(fragments, layer_rank, pixel_count, slot_count, block_run, brick_order, interlace):
    owners, capacity, width = fragments.shape[2], fragments.shape[3], fragments.shape[-1]
    runs_total = interlace.shape[0]
    depths, tiles, bricks = (lax.axis_size(a) for a in ("depth", "tile", "brick"))
    share = runs_total // depths
    blocks = depths * owners * capacity
    lanes = min(128, runs_total)
    args = [
        fragments.reshape(owners * capacity * 16, width),
        layer_rank.reshape(owners * capacity * 4, width),
        pixel_count.reshape(owners, capacity).T,
        slot_count.reshape(1, owners),
        block_run.reshape(owners, capacity).T,
        brick_order.reshape(1, owners),
        interlace.reshape(runs_total // lanes, lanes),
    ]
    vmem = pl.BlockSpec(memory_space=pltpu.VMEM)
    recv, earlier, target = pl.pallas_call(
        functools.partial(exchange, (depths, tiles, bricks, owners, capacity, share)),
        out_shape=(
            jax.ShapeDtypeStruct((blocks * 4, width), F32),
            jax.ShapeDtypeStruct((blocks, 2 * blocks), BF16),
            jax.ShapeDtypeStruct((share, 2 * blocks), BF16),
        ),
        in_specs=[pl.BlockSpec(memory_space=pltpu.HBM)] * len(args),
        out_specs=(vmem, vmem, vmem),
        scratch_shapes=[pltpu.VMEM(a.shape, a.dtype) for a in args]
        + [
            pltpu.VMEM((owners * capacity * 4, width), F32),
            pltpu.VMEM((depths, 8, 2 * blocks), F32),
            pltpu.SemaphoreType.DMA((len(args),)),
            pltpu.SemaphoreType.DMA,
            pltpu.SemaphoreType.DMA((tiles,)),
            pltpu.SemaphoreType.DMA,
            pltpu.SemaphoreType.DMA,
            pltpu.SemaphoreType.DMA,
            pltpu.SemaphoreType.DMA,
        ],
        compiler_params=pltpu.CompilerParams(
            collective_id=0, has_side_effects=True, vmem_limit_bytes=32 * 1024 * 1024
        ),
        name="exchange",
    )(*[pltpu.with_memory_space_constraint(a, pltpu.HBM) for a in args])
    image = pl.pallas_call(
        compose,
        out_shape=jax.ShapeDtypeStruct((share * 4, width), F32),
        in_specs=[vmem] * 3,
        out_specs=vmem,
        compiler_params=pltpu.CompilerParams(vmem_limit_bytes=32 * 1024 * 1024),
        name="compose",
    )(recv, earlier, target)
    return image.reshape(1, 1, share, 4, width)


def solution(mesh):
    return jax.shard_map(
        shards,
        mesh=mesh,
        in_specs=(
            P("depth", ("tile", "brick"), None, None, None, None),
            P("depth", ("tile", "brick"), None, None, None, None),
            P("depth", ("tile", "brick"), None, None),
            P("depth", ("tile", "brick"), None),
            P("depth", ("tile", "brick"), None, None),
            P("depth", None),
            P(),
        ),
        out_specs=P(("tile", "brick"), "depth", None, None, None),
        check_vma=False,
    )
```

```python
import functools

import jax
import jax.numpy as jnp
from jax import lax
from jax.experimental import pallas as pl
from jax.experimental.pallas import tpu as pltpu
from jax.sharding import PartitionSpec as P

MESH = pl.DeviceIdType.MESH
F32 = jnp.float32
BF16 = jnp.bfloat16


def iota(shape, dim):
    return lax.broadcasted_iota(jnp.int32, shape, dim)


def log2(n):
    assert n & (n - 1) == 0
    return n.bit_length() - 1


def column(row, rows):
    shape = (rows, row.shape[1])
    return jnp.sum(jnp.where(iota(shape, 0) == iota(shape, 1), row, 0.0), axis=1, keepdims=True)


def split(x):
    high = x.astype(BF16)
    low = (x - high.astype(F32)).astype(BF16)
    return jnp.concatenate([high, low], axis=0)


def blend(frag, rank, limits, send, owners, capacity):
    pixel = iota((owners, frag.shape[-1]), 1).astype(F32)
    for slot in range(capacity):
        ranks = [rank[pl.ds(slot * 4 + l, owners, stride=capacity * 4), :] for l in range(4)]
        value = [
            [frag[pl.ds(slot * 16 + l * 4 + e, owners, stride=capacity * 16), :] for e in range(4)]
            for l in range(4)
        ]
        clear = [1.0 - value[l][3] for l in range(4)]
        through = [None] * 4
        for l in range(4):
            for m in range(l):
                front = ranks[m] < ranks[l]
                behind = jnp.where(front, clear[m], 1.0)
                ahead = jnp.where(front, 1.0, clear[l])
                through[l] = behind if through[l] is None else through[l] * behind
                through[m] = ahead if through[m] is None else through[m] * ahead
        visible = pixel < limits[slot]
        for e in range(4):
            total = value[0][e] * through[0]
            for l in range(1, 4):
                total = total + value[l][e] * through[l]
            send[pl.ds(slot * 4 + e, owners, stride=capacity * 4), :] = jnp.where(visible, total, 0.0)


def describe(slots, runs, order, place, blocks, owners, capacity, meta):
    width = meta.shape[1]
    lane = iota((owners, width), 1) & (blocks - 1)
    own = (lane >> log2(owners * capacity)) == place
    brick = (lane >> log2(capacity)) & (owners - 1)
    slot = lane & (capacity - 1)
    chosen = own & (brick == iota((owners, width), 0))
    live = slot.astype(F32) < column(slots.astype(F32), owners)
    runs = runs.astype(F32)
    run = jnp.broadcast_to(column(runs[0:1, :], owners), (owners, width))
    for c in range(1, capacity):
        run = jnp.where(slot == c, column(runs[c : c + 1, :], owners), run)
    key = jnp.sum(jnp.where(chosen & live, run + 1.0, 0.0), axis=0, keepdims=True)
    depth = column(order.astype(F32), owners) + (place * owners).astype(F32)
    rank = jnp.sum(jnp.where(chosen, depth, 0.0), axis=0, keepdims=True)
    row = iota(meta.shape, 0)
    meta[...] = jnp.where(row == 0, key, jnp.where(row == 1, rank, 0.0))


def exchange(sizes, frag_hbm, rank_hbm, count_hbm, slots_hbm, runs_hbm, order_hbm, lace_hbm,
             recv, earlier, target,
             frag, rank, count, slots, runs, order, lace, send, meta,
             load_sem, send_sem, recv_sem, meta_send, meta_recv):
    depths, tiles, bricks, owners, capacity, share = sizes
    d, t, b = lax.axis_index("depth"), lax.axis_index("tile"), lax.axis_index("brick")
    blocks = depths * owners * capacity
    group = capacity * 4

    loads = [
        pltpu.make_async_copy(src, dst, load_sem.at[i])
        for i, (src, dst) in enumerate([
            (frag_hbm, frag), (rank_hbm, rank), (count_hbm, count), (slots_hbm, slots),
            (runs_hbm, runs), (order_hbm, order), (lace_hbm, lace),
        ])
    ]
    for load in loads:
        load.start()

    def away(own, k):
        for bit in range(k.bit_length()):
            if k >> bit & 1:
                own = own + (1 - 2 * ((own // (1 << bit)) % 2)) * (1 << bit)
        return own

    half = tiles // 2
    far = list(range(half, tiles)) + list(range(half - 1, -1, -1))
    mates = [
        (away(d, kd), away(t, kt), away(b, kb))
        for kt in far for kb in range(bricks) for kd in range(depths) if kt or kb or kd
    ]
    partners = [(away(d, kd), t, b) for kd in range(1, depths)]
    barrier = pltpu.get_barrier_semaphore()
    for to in mates:
        pl.semaphore_signal(barrier, inc=1, device_id=to, device_id_type=MESH)

    for load in loads[2:]:
        load.wait()
    describe(slots[...], runs[...], order[...], d, blocks, owners, capacity, meta.at[d])
    limit = count[...].astype(F32)
    limits = [column(limit[c : c + 1, :], owners) for c in range(capacity)]
    loads[0].wait()
    loads[1].wait()
    blend(frag, rank, limits, send, owners, capacity)
    mine = t * bricks + b
    source = pl.ds(pl.multiple_of((d * owners + mine) * group, group), group)

    pl.semaphore_wait(barrier, len(mates))

    for to in partners:
        pltpu.make_async_remote_copy(
            src_ref=meta.at[d], dst_ref=meta.at[d], send_sem=meta_send, recv_sem=meta_recv,
            device_id=to, device_id_type=MESH,
        ).start()
    for to in mates:
        owner = to[1] * bricks + to[2]
        pltpu.make_async_remote_copy(
            src_ref=send.at[pl.ds(pl.multiple_of(owner * group, group), group)],
            dst_ref=recv.at[source], send_sem=send_sem, recv_sem=recv_sem,
            device_id=to, device_id_type=MESH,
        ).start()
    recv[source, :] = send[pl.ds(pl.multiple_of(mine * group, group), group), :]

    slots_total = lace.shape[0] * lace.shape[1]
    place = lace[...] - d * share
    shown = jnp.concatenate(
        [
            jnp.where(place[i : i + 1, :] == iota((share, lace.shape[1]), 0), 1.0, 0.0)
            for i in range(lace.shape[0])
        ],
        axis=1,
    ).astype(BF16)

    if partners:
        part = meta.at[pl.ds(0, depths - 1)]
        pltpu.make_async_copy(part, part, meta_recv).wait()
    known = meta[0]
    for s in range(1, depths):
        known = known + meta[s]
    key, rank_row = known[0:1, :], known[1:2, :]
    same = column(key, blocks) == key
    before = rank_row < column(rank_row, blocks)
    earlier[...] = jnp.where(same & before, 1.0, 0.0).astype(BF16)
    holds = iota((slots_total, 2 * blocks), 0).astype(F32) + 1.0 == key
    target[...] = jnp.dot(
        shown, jnp.where(holds, 1.0, 0.0).astype(BF16), preferred_element_type=F32
    ).astype(BF16)

    whole = recv.at[pl.ds(0, len(mates) * group)]
    pltpu.make_async_copy(whole, whole, recv_sem).wait()
    pltpu.make_async_copy(whole, whole, send_sem).wait()
    if partners:
        pltpu.make_async_copy(part, part, meta_send).wait()


def compose(recv, earlier, target, out):
    blocks = earlier.shape[0]
    share = target.shape[0]
    clear = jnp.log(1.0 - recv[pl.ds(3, blocks, stride=4), :])
    passed = jnp.exp(jnp.dot(earlier[...], split(clear), preferred_element_type=F32))
    for e in range(4):
        shaded = recv[pl.ds(e, blocks, stride=4), :] * passed
        out[pl.ds(e, share, stride=4), :] = jnp.dot(
            target[...], split(shaded), preferred_element_type=F32
        )


def shards(fragments, layer_rank, pixel_count, slot_count, block_run, brick_order, interlace):
    owners, capacity, width = fragments.shape[2], fragments.shape[3], fragments.shape[-1]
    runs_total = interlace.shape[0]
    depths, tiles, bricks = (lax.axis_size(a) for a in ("depth", "tile", "brick"))
    share = runs_total // depths
    blocks = depths * owners * capacity
    lanes = min(128, runs_total)
    args = [
        fragments.reshape(owners * capacity * 16, width),
        layer_rank.reshape(owners * capacity * 4, width),
        pixel_count.reshape(owners, capacity).T,
        slot_count.reshape(1, owners),
        block_run.reshape(owners, capacity).T,
        brick_order.reshape(1, owners),
        interlace.reshape(runs_total // lanes, lanes),
    ]
    vmem = pl.BlockSpec(memory_space=pltpu.VMEM)
    recv, earlier, target = pl.pallas_call(
        functools.partial(exchange, (depths, tiles, bricks, owners, capacity, share)),
        out_shape=(
            jax.ShapeDtypeStruct((blocks * 4, width), F32),
            jax.ShapeDtypeStruct((blocks, 2 * blocks), BF16),
            jax.ShapeDtypeStruct((share, 2 * blocks), BF16),
        ),
        in_specs=[pl.BlockSpec(memory_space=pltpu.HBM)] * len(args),
        out_specs=(vmem, vmem, vmem),
        scratch_shapes=[pltpu.VMEM(a.shape, a.dtype) for a in args]
        + [
            pltpu.VMEM((owners * capacity * 4, width), F32),
            pltpu.VMEM((depths, 8, 2 * blocks), F32),
            pltpu.SemaphoreType.DMA((len(args),)),
            pltpu.SemaphoreType.DMA,
            pltpu.SemaphoreType.DMA,
            pltpu.SemaphoreType.DMA,
            pltpu.SemaphoreType.DMA,
        ],
        compiler_params=pltpu.CompilerParams(
            collective_id=0, has_side_effects=True, vmem_limit_bytes=32 * 1024 * 1024
        ),
        name="exchange",
    )(*[pltpu.with_memory_space_constraint(a, pltpu.HBM) for a in args])
    image = pl.pallas_call(
        compose,
        out_shape=jax.ShapeDtypeStruct((share * 4, width), F32),
        in_specs=[vmem] * 3,
        out_specs=vmem,
        compiler_params=pltpu.CompilerParams(vmem_limit_bytes=32 * 1024 * 1024),
        name="compose",
    )(recv, earlier, target)
    return image.reshape(1, 1, share, 4, width)


def solution(mesh):
    return jax.shard_map(
        shards,
        mesh=mesh,
        in_specs=(
            P("depth", ("tile", "brick"), None, None, None, None),
            P("depth", ("tile", "brick"), None, None, None, None),
            P("depth", ("tile", "brick"), None, None),
            P("depth", ("tile", "brick"), None),
            P("depth", ("tile", "brick"), None, None),
            P("depth", None),
            P(),
        ),
        out_specs=P(("tile", "brick"), "depth", None, None, None),
        check_vma=False,
    )
```

```python
import functools

import jax
import jax.numpy as jnp
from jax import lax
from jax.experimental import pallas as pl
from jax.experimental.pallas import tpu as pltpu
from jax.sharding import PartitionSpec as P

MESH = pl.DeviceIdType.MESH
F32 = jnp.float32
BF16 = jnp.bfloat16


def iota(shape, dim):
    return lax.broadcasted_iota(jnp.int32, shape, dim)


def log2(n):
    assert n & (n - 1) == 0
    return n.bit_length() - 1


def column(row, rows, first=0):
    shape = (rows, row.shape[1])
    taken = iota(shape, 0) + first == iota(shape, 1)
    return jnp.sum(jnp.where(taken, row, 0.0), axis=1, keepdims=True)


def split(x):
    high = x.astype(BF16)
    low = (x - high.astype(F32)).astype(BF16)
    return jnp.concatenate([high, low], axis=0)


def blend(frag, rank, limits, send, first, owners, capacity):
    pixel = iota((owners, frag.shape[-1]), 1).astype(F32)
    for slot in range(capacity):
        ranks = [rank[pl.ds((first * capacity + slot) * 4 + l, owners, stride=capacity * 4), :] for l in range(4)]
        value = [
            [
                frag[pl.ds((first * capacity + slot) * 16 + l * 4 + e, owners, stride=capacity * 16), :]
                for e in range(4)
            ]
            for l in range(4)
        ]
        clear = [1.0 - value[l][3] for l in range(4)]
        through = [None] * 4
        for l in range(4):
            for m in range(l):
                front = ranks[m] < ranks[l]
                behind = jnp.where(front, clear[m], 1.0)
                ahead = jnp.where(front, 1.0, clear[l])
                through[l] = behind if through[l] is None else through[l] * behind
                through[m] = ahead if through[m] is None else through[m] * ahead
        visible = pixel < limits[slot]
        for e in range(4):
            total = value[0][e] * through[0]
            for l in range(1, 4):
                total = total + value[l][e] * through[l]
            rows = pl.ds((first * capacity + slot) * 4 + e, owners, stride=capacity * 4)
            send[rows, :] = jnp.where(visible, total, 0.0)


def describe(slots, runs, order, place, blocks, owners, capacity, meta):
    width = meta.shape[1]
    lane = iota((owners, width), 1) & (blocks - 1)
    own = (lane >> log2(owners * capacity)) == place
    brick = (lane >> log2(capacity)) & (owners - 1)
    slot = lane & (capacity - 1)
    chosen = own & (brick == iota((owners, width), 0))
    live = slot.astype(F32) < column(slots.astype(F32), owners)
    runs = runs.astype(F32)
    run = jnp.broadcast_to(column(runs[0:1, :], owners), (owners, width))
    for c in range(1, capacity):
        run = jnp.where(slot == c, column(runs[c : c + 1, :], owners), run)
    key = jnp.sum(jnp.where(chosen & live, run + 1.0, 0.0), axis=0, keepdims=True)
    depth = column(order.astype(F32), owners) + (place * owners).astype(F32)
    rank = jnp.sum(jnp.where(chosen, depth, 0.0), axis=0, keepdims=True)
    row = iota(meta.shape, 0)
    meta[...] = jnp.where(row == 0, key, jnp.where(row == 1, rank, 0.0))


def exchange(sizes, frag_hbm, rank_hbm, count_hbm, slots_hbm, runs_hbm, order_hbm, lace_hbm,
             recv, earlier, target,
             frag, rank, count, slots, runs, order, lace, send, meta,
             load_sem, send_sem, recv_sem, meta_send, meta_recv):
    depths, tiles, bricks, owners, capacity, share = sizes
    d, t, b = lax.axis_index("depth"), lax.axis_index("tile"), lax.axis_index("brick")
    blocks = depths * owners * capacity
    group = capacity * 4

    half = tiles // 2
    part = half * bricks
    side = t // half
    firsts = [(1 - side) * part, side * part]

    def piece(src, dst, rows, h, sem):
        start = pl.multiple_of(firsts[h] * rows, part * rows)
        return pltpu.make_async_copy(
            src.at[pl.ds(start, part * rows)], dst.at[pl.ds(h * part * rows, part * rows)], sem
        )

    large = [
        [
            piece(frag_hbm, frag, capacity * 16, h, load_sem.at[2 * h]),
            piece(rank_hbm, rank, capacity * 4, h, load_sem.at[2 * h + 1]),
        ]
        for h in range(2)
    ]
    counts = pltpu.make_async_copy(count_hbm, count, load_sem.at[4])
    small = [
        pltpu.make_async_copy(src, dst, load_sem.at[5 + i])
        for i, (src, dst) in enumerate([
            (slots_hbm, slots), (runs_hbm, runs), (order_hbm, order), (lace_hbm, lace),
        ])
    ]
    for load in large[0] + [counts] + large[1]:
        load.start()

    def away(own, k):
        for bit in range(k.bit_length()):
            if k >> bit & 1:
                own = own + (1 - 2 * ((own // (1 << bit)) % 2)) * (1 << bit)
        return own

    mates = [[], []]
    for kt in list(range(half, tiles)) + list(range(half - 1, -1, -1)):
        for kb in range(bricks):
            for kd in range(depths):
                if kt or kb or kd:
                    mates[kt < half].append((away(d, kd), away(t, kt), away(b, kb)))
    partners = [(away(d, kd), t, b) for kd in range(1, depths)]
    others = len(mates[0]) + len(mates[1])
    barrier = pltpu.get_barrier_semaphore()
    for to in mates[0] + mates[1]:
        pl.semaphore_signal(barrier, inc=1, device_id=to, device_id_type=MESH)
    for load in small:
        load.start()

    mine = t * bricks + b
    source = pl.ds(pl.multiple_of((d * owners + mine) * group, group), group)

    def outgoing(h, tile, brick):
        at = h * part + (tile % half) * bricks + brick
        return pl.ds(pl.multiple_of(at * group, group), group)

    counts.wait()
    limit = count[...].astype(F32)
    limits = [
        [column(limit[c : c + 1, :], part, firsts[h]) for c in range(capacity)] for h in range(2)
    ]
    for h in range(2):
        for load in large[h]:
            load.wait()
        blend(frag, rank, limits[h], send, h * part, part, capacity)
        if h == 0:
            pl.semaphore_wait(barrier, others)
        for to in mates[h]:
            pltpu.make_async_remote_copy(
                src_ref=send.at[outgoing(h, to[1], to[2])],
                dst_ref=recv.at[source], send_sem=send_sem, recv_sem=recv_sem,
                device_id=to, device_id_type=MESH,
            ).start()

    for load in small:
        load.wait()
    describe(slots[...], runs[...], order[...], d, blocks, owners, capacity, meta.at[d])
    for to in partners:
        pltpu.make_async_remote_copy(
            src_ref=meta.at[d], dst_ref=meta.at[d], send_sem=meta_send, recv_sem=meta_recv,
            device_id=to, device_id_type=MESH,
        ).start()
    recv[source, :] = send[outgoing(1, t, b), :]

    slots_total = lace.shape[0] * lace.shape[1]
    place = lace[...] - d * share
    shown = jnp.concatenate(
        [
            jnp.where(place[i : i + 1, :] == iota((share, lace.shape[1]), 0), 1.0, 0.0)
            for i in range(lace.shape[0])
        ],
        axis=1,
    ).astype(BF16)

    if partners:
        told = meta.at[pl.ds(0, depths - 1)]
        pltpu.make_async_copy(told, told, meta_recv).wait()
    known = meta[0]
    for s in range(1, depths):
        known = known + meta[s]
    key, rank_row = known[0:1, :], known[1:2, :]
    same = column(key, blocks) == key
    before = rank_row < column(rank_row, blocks)
    earlier[...] = jnp.where(same & before, 1.0, 0.0).astype(BF16)
    holds = iota((slots_total, 2 * blocks), 0).astype(F32) + 1.0 == key
    target[...] = jnp.dot(
        shown, jnp.where(holds, 1.0, 0.0).astype(BF16), preferred_element_type=F32
    ).astype(BF16)

    whole = recv.at[pl.ds(0, others * group)]
    pltpu.make_async_copy(whole, whole, recv_sem).wait()
    pltpu.make_async_copy(whole, whole, send_sem).wait()
    if partners:
        pltpu.make_async_copy(told, told, meta_send).wait()


def compose(recv, earlier, target, out, image, sem):
    blocks = earlier.shape[0]
    share = target.shape[0]
    clear = jnp.log(1.0 - recv[pl.ds(3, blocks, stride=4), :])
    passed = jnp.exp(jnp.dot(earlier[...], split(clear), preferred_element_type=F32))
    shaded = jnp.concatenate(
        [split(recv[pl.ds(e, blocks, stride=4), :] * passed) for e in range(4)], axis=1
    )
    width = recv.shape[1]
    pieces = sem.shape[0]
    rows = share // pieces
    writes = []
    for i in range(pieces):
        part = jnp.dot(
            target[i * rows : (i + 1) * rows, :], shaded, preferred_element_type=F32
        )
        for e in range(4):
            image[pl.ds(i * rows * 4 + e, rows, stride=4), :] = part[:, e * width : (e + 1) * width]
        where = pl.ds(i * rows * 4, rows * 4)
        writes.append(pltpu.make_async_copy(image.at[where], out.at[where], sem.at[i]))
        writes[-1].start()
    for write in writes:
        write.wait()


def shards(fragments, layer_rank, pixel_count, slot_count, block_run, brick_order, interlace):
    owners, capacity, width = fragments.shape[2], fragments.shape[3], fragments.shape[-1]
    runs_total = interlace.shape[0]
    depths, tiles, bricks = (lax.axis_size(a) for a in ("depth", "tile", "brick"))
    share = runs_total // depths
    blocks = depths * owners * capacity
    lanes = min(128, runs_total)
    args = [
        fragments.reshape(owners * capacity * 16, width),
        layer_rank.reshape(owners * capacity * 4, width),
        pixel_count.reshape(owners, capacity).T,
        slot_count.reshape(1, owners),
        block_run.reshape(owners, capacity).T,
        brick_order.reshape(1, owners),
        interlace.reshape(runs_total // lanes, lanes),
    ]
    vmem = pl.BlockSpec(memory_space=pltpu.VMEM)
    recv, earlier, target = pl.pallas_call(
        functools.partial(exchange, (depths, tiles, bricks, owners, capacity, share)),
        out_shape=(
            jax.ShapeDtypeStruct((blocks * 4, width), F32),
            jax.ShapeDtypeStruct((blocks, 2 * blocks), BF16),
            jax.ShapeDtypeStruct((share, 2 * blocks), BF16),
        ),
        in_specs=[pl.BlockSpec(memory_space=pltpu.HBM)] * len(args),
        out_specs=(vmem, vmem, vmem),
        scratch_shapes=[pltpu.VMEM(a.shape, a.dtype) for a in args]
        + [
            pltpu.VMEM((owners * capacity * 4, width), F32),
            pltpu.VMEM((depths, 8, 2 * blocks), F32),
            pltpu.SemaphoreType.DMA((len(args) + 2,)),
            pltpu.SemaphoreType.DMA,
            pltpu.SemaphoreType.DMA,
            pltpu.SemaphoreType.DMA,
            pltpu.SemaphoreType.DMA,
        ],
        compiler_params=pltpu.CompilerParams(
            collective_id=0, has_side_effects=True, vmem_limit_bytes=32 * 1024 * 1024
        ),
        name="exchange",
    )(*[pltpu.with_memory_space_constraint(a, pltpu.HBM) for a in args])
    image = pl.pallas_call(
        compose,
        out_shape=jax.ShapeDtypeStruct((share * 4, width), F32),
        in_specs=[vmem] * 3,
        out_specs=pl.BlockSpec(memory_space=pl.ANY),
        scratch_shapes=[
            pltpu.VMEM((share * 4, width), F32),
            pltpu.SemaphoreType.DMA((max(1, share // 32),)),
        ],
        compiler_params=pltpu.CompilerParams(vmem_limit_bytes=32 * 1024 * 1024),
        name="compose",
    )(recv, earlier, target)
    return image.reshape(1, 1, share, 4, width)


def solution(mesh):
    return jax.shard_map(
        shards,
        mesh=mesh,
        in_specs=(
            P("depth", ("tile", "brick"), None, None, None, None),
            P("depth", ("tile", "brick"), None, None, None, None),
            P("depth", ("tile", "brick"), None, None),
            P("depth", ("tile", "brick"), None),
            P("depth", ("tile", "brick"), None, None),
            P("depth", None),
            P(),
        ),
        out_specs=P(("tile", "brick"), "depth", None, None, None),
        check_vma=False,
    )
```

```python
import functools

import jax
import jax.numpy as jnp
from jax import lax
from jax.experimental import pallas as pl
from jax.experimental.pallas import tpu as pltpu
from jax.sharding import PartitionSpec as P

MESH = pl.DeviceIdType.MESH
F32 = jnp.float32
BF16 = jnp.bfloat16


def iota(shape, dim):
    return lax.broadcasted_iota(jnp.int32, shape, dim)


def log2(n):
    assert n & (n - 1) == 0
    return n.bit_length() - 1


def column(row, rows, first=0):
    shape = (rows, row.shape[1])
    taken = iota(shape, 0) + first == iota(shape, 1)
    return jnp.sum(jnp.where(taken, row, 0.0), axis=1, keepdims=True)


def split(x):
    high = x.astype(BF16)
    low = (x - high.astype(F32)).astype(BF16)
    return jnp.concatenate([high, low], axis=0)


def blend(frag, rank, limits, send, first, owners, capacity):
    pixel = iota((owners, frag.shape[-1]), 1).astype(F32)
    for slot in range(capacity):
        ranks = [rank[pl.ds((first * capacity + slot) * 4 + l, owners, stride=capacity * 4), :] for l in range(4)]
        value = [
            [
                frag[pl.ds((first * capacity + slot) * 16 + l * 4 + e, owners, stride=capacity * 16), :]
                for e in range(4)
            ]
            for l in range(4)
        ]
        clear = [1.0 - value[l][3] for l in range(4)]
        through = [None] * 4
        for l in range(4):
            for m in range(l):
                front = ranks[m] < ranks[l]
                behind = jnp.where(front, clear[m], 1.0)
                ahead = jnp.where(front, 1.0, clear[l])
                through[l] = behind if through[l] is None else through[l] * behind
                through[m] = ahead if through[m] is None else through[m] * ahead
        visible = pixel < limits[slot]
        for e in range(4):
            total = value[0][e] * through[0]
            for l in range(1, 4):
                total = total + value[l][e] * through[l]
            rows = pl.ds((first * capacity + slot) * 4 + e, owners, stride=capacity * 4)
            send[rows, :] = jnp.where(visible, total, 0.0)


def describe(slots, runs, order, place, blocks, owners, capacity, meta):
    width = meta.shape[1]
    lane = iota((owners, width), 1) & (blocks - 1)
    own = (lane >> log2(owners * capacity)) == place
    brick = (lane >> log2(capacity)) & (owners - 1)
    slot = lane & (capacity - 1)
    chosen = own & (brick == iota((owners, width), 0))
    live = slot.astype(F32) < column(slots.astype(F32), owners)
    runs = runs.astype(F32)
    run = jnp.broadcast_to(column(runs[0:1, :], owners), (owners, width))
    for c in range(1, capacity):
        run = jnp.where(slot == c, column(runs[c : c + 1, :], owners), run)
    key = jnp.sum(jnp.where(chosen & live, run + 1.0, 0.0), axis=0, keepdims=True)
    depth = column(order.astype(F32), owners) + (place * owners).astype(F32)
    rank = jnp.sum(jnp.where(chosen, depth, 0.0), axis=0, keepdims=True)
    row = iota(meta.shape, 0)
    meta[...] = jnp.where(row == 0, key, jnp.where(row == 1, rank, 0.0))


def exchange(sizes, frag_hbm, rank_hbm, count_hbm, slots_hbm, runs_hbm, order_hbm, lace_hbm,
             recv, earlier, target,
             frag, rank, count, slots, runs, order, lace, send, meta,
             load_sem, send_sem, recv_sem, meta_send, meta_recv):
    depths, tiles, bricks, owners, capacity, share = sizes
    d, t, b = lax.axis_index("depth"), lax.axis_index("tile"), lax.axis_index("brick")
    blocks = depths * owners * capacity
    group = capacity * 4

    half = tiles // 2
    part = half * bricks
    side = t // half
    firsts = [(1 - side) * part, side * part]

    def piece(src, dst, rows, h, sem):
        start = pl.multiple_of(firsts[h] * rows, part * rows)
        return pltpu.make_async_copy(
            src.at[pl.ds(start, part * rows)], dst.at[pl.ds(h * part * rows, part * rows)], sem
        )

    large = [
        [
            piece(frag_hbm, frag, capacity * 16, h, load_sem.at[2 * h]),
            piece(rank_hbm, rank, capacity * 4, h, load_sem.at[2 * h + 1]),
        ]
        for h in range(2)
    ]
    counts = pltpu.make_async_copy(count_hbm, count, load_sem.at[4])
    small = [
        pltpu.make_async_copy(src, dst, load_sem.at[5 + i])
        for i, (src, dst) in enumerate([
            (slots_hbm, slots), (runs_hbm, runs), (order_hbm, order), (lace_hbm, lace),
        ])
    ]
    def away(own, k):
        for bit in range(k.bit_length()):
            if k >> bit & 1:
                own = own + (1 - 2 * ((own // (1 << bit)) % 2)) * (1 << bit)
        return own

    mates = [[], []]
    for kt in list(range(half, tiles)) + list(range(half - 1, -1, -1)):
        for kb in range(bricks):
            for kd in range(depths):
                if kt or kb or kd:
                    mates[kt < half].append((away(d, kd), away(t, kt), away(b, kb)))
    partners = [(away(d, kd), t, b) for kd in range(1, depths)]
    others = len(mates[0]) + len(mates[1])
    barrier = pltpu.get_barrier_semaphore()
    for to in mates[0] + mates[1]:
        pl.semaphore_signal(barrier, inc=1, device_id=to, device_id_type=MESH)
    for load in small[:3] + [counts] + large[0] + large[1] + small[3:]:
        load.start()

    mine = t * bricks + b
    source = pl.ds(pl.multiple_of((d * owners + mine) * group, group), group)

    def outgoing(h, tile, brick):
        at = h * part + (tile % half) * bricks + brick
        return pl.ds(pl.multiple_of(at * group, group), group)

    for load in small[:3] + [counts]:
        load.wait()
    describe(slots[...], runs[...], order[...], d, blocks, owners, capacity, meta.at[d])
    limit = count[...].astype(F32)
    for h in range(2):
        limits = [column(limit[c : c + 1, :], part, firsts[h]) for c in range(capacity)]
        for load in large[h]:
            load.wait()
        blend(frag, rank, limits, send, h * part, part, capacity)

    pl.semaphore_wait(barrier, others)
    for to in partners:
        pltpu.make_async_remote_copy(
            src_ref=meta.at[d], dst_ref=meta.at[d], send_sem=meta_send, recv_sem=meta_recv,
            device_id=to, device_id_type=MESH,
        ).start()
    for h in range(2):
        for to in mates[h]:
            pltpu.make_async_remote_copy(
                src_ref=send.at[outgoing(h, to[1], to[2])],
                dst_ref=recv.at[source], send_sem=send_sem, recv_sem=recv_sem,
                device_id=to, device_id_type=MESH,
            ).start()
    small[3].wait()
    recv[source, :] = send[outgoing(1, t, b), :]

    slots_total = lace.shape[0] * lace.shape[1]
    place = lace[...] - d * share
    shown = jnp.concatenate(
        [
            jnp.where(place[i : i + 1, :] == iota((share, lace.shape[1]), 0), 1.0, 0.0)
            for i in range(lace.shape[0])
        ],
        axis=1,
    ).astype(BF16)

    if partners:
        told = meta.at[pl.ds(0, depths - 1)]
        pltpu.make_async_copy(told, told, meta_recv).wait()
    known = meta[0]
    for s in range(1, depths):
        known = known + meta[s]
    key, rank_row = known[0:1, :], known[1:2, :]
    same = column(key, blocks) == key
    before = rank_row < column(rank_row, blocks)
    earlier[...] = jnp.where(same & before, 1.0, 0.0).astype(BF16)
    holds = iota((slots_total, 2 * blocks), 0).astype(F32) + 1.0 == key
    target[...] = jnp.dot(
        shown, jnp.where(holds, 1.0, 0.0).astype(BF16), preferred_element_type=F32
    ).astype(BF16)

    whole = recv.at[pl.ds(0, others * group)]
    pltpu.make_async_copy(whole, whole, recv_sem).wait()
    pltpu.make_async_copy(whole, whole, send_sem).wait()
    if partners:
        pltpu.make_async_copy(told, told, meta_send).wait()


def compose(recv, earlier, target, out, image, sem):
    blocks = earlier.shape[0]
    share = target.shape[0]
    clear = jnp.log(1.0 - recv[pl.ds(3, blocks, stride=4), :])
    passed = jnp.exp(jnp.dot(earlier[...], split(clear), preferred_element_type=F32))
    shaded = jnp.concatenate(
        [split(recv[pl.ds(e, blocks, stride=4), :] * passed) for e in range(4)], axis=1
    )
    width = recv.shape[1]
    pieces = sem.shape[0]
    rows = share // pieces
    writes = []
    for i in range(pieces):
        part = jnp.dot(
            target[i * rows : (i + 1) * rows, :], shaded, preferred_element_type=F32
        )
        for e in range(4):
            image[pl.ds(i * rows * 4 + e, rows, stride=4), :] = part[:, e * width : (e + 1) * width]
        where = pl.ds(i * rows * 4, rows * 4)
        writes.append(pltpu.make_async_copy(image.at[where], out.at[where], sem.at[i]))
        writes[-1].start()
    for write in writes:
        write.wait()


def shards(fragments, layer_rank, pixel_count, slot_count, block_run, brick_order, interlace):
    owners, capacity, width = fragments.shape[2], fragments.shape[3], fragments.shape[-1]
    runs_total = interlace.shape[0]
    depths, tiles, bricks = (lax.axis_size(a) for a in ("depth", "tile", "brick"))
    share = runs_total // depths
    blocks = depths * owners * capacity
    lanes = min(128, runs_total)
    args = [
        fragments.reshape(owners * capacity * 16, width),
        layer_rank.reshape(owners * capacity * 4, width),
        pixel_count.reshape(owners, capacity).T,
        slot_count.reshape(1, owners),
        block_run.reshape(owners, capacity).T,
        brick_order.reshape(1, owners),
        interlace.reshape(runs_total // lanes, lanes),
    ]
    vmem = pl.BlockSpec(memory_space=pltpu.VMEM)
    recv, earlier, target = pl.pallas_call(
        functools.partial(exchange, (depths, tiles, bricks, owners, capacity, share)),
        out_shape=(
            jax.ShapeDtypeStruct((blocks * 4, width), F32),
            jax.ShapeDtypeStruct((blocks, 2 * blocks), BF16),
            jax.ShapeDtypeStruct((share, 2 * blocks), BF16),
        ),
        in_specs=[pl.BlockSpec(memory_space=pltpu.HBM)] * len(args),
        out_specs=(vmem, vmem, vmem),
        scratch_shapes=[pltpu.VMEM(a.shape, a.dtype) for a in args]
        + [
            pltpu.VMEM((owners * capacity * 4, width), F32),
            pltpu.VMEM((depths, 8, 2 * blocks), F32),
            pltpu.SemaphoreType.DMA((len(args) + 2,)),
            pltpu.SemaphoreType.DMA,
            pltpu.SemaphoreType.DMA,
            pltpu.SemaphoreType.DMA,
            pltpu.SemaphoreType.DMA,
        ],
        compiler_params=pltpu.CompilerParams(
            collective_id=0, has_side_effects=True, vmem_limit_bytes=32 * 1024 * 1024
        ),
        name="exchange",
    )(*[pltpu.with_memory_space_constraint(a, pltpu.HBM) for a in args])
    image = pl.pallas_call(
        compose,
        out_shape=jax.ShapeDtypeStruct((share * 4, width), F32),
        in_specs=[vmem] * 3,
        out_specs=pl.BlockSpec(memory_space=pl.ANY),
        scratch_shapes=[
            pltpu.VMEM((share * 4, width), F32),
            pltpu.SemaphoreType.DMA((max(1, share // 32),)),
        ],
        compiler_params=pltpu.CompilerParams(vmem_limit_bytes=32 * 1024 * 1024),
        name="compose",
    )(recv, earlier, target)
    return image.reshape(1, 1, share, 4, width)


def solution(mesh):
    return jax.shard_map(
        shards,
        mesh=mesh,
        in_specs=(
            P("depth", ("tile", "brick"), None, None, None, None),
            P("depth", ("tile", "brick"), None, None, None, None),
            P("depth", ("tile", "brick"), None, None),
            P("depth", ("tile", "brick"), None),
            P("depth", ("tile", "brick"), None, None),
            P("depth", None),
            P(),
        ),
        out_specs=P(("tile", "brick"), "depth", None, None, None),
        check_vma=False,
    )
```

```python
import functools

import jax
import jax.numpy as jnp
from jax import lax
from jax.experimental import pallas as pl
from jax.experimental.pallas import tpu as pltpu
from jax.sharding import PartitionSpec as P

MESH = pl.DeviceIdType.MESH
F32 = jnp.float32
BF16 = jnp.bfloat16


def iota(shape, dim):
    return lax.broadcasted_iota(jnp.int32, shape, dim)


def log2(n):
    assert n & (n - 1) == 0
    return n.bit_length() - 1


def column(row, rows, first=0):
    shape = (rows, row.shape[1])
    taken = iota(shape, 0) + first == iota(shape, 1)
    return jnp.sum(jnp.where(taken, row, 0.0), axis=1, keepdims=True)


def split(x):
    high = x.astype(BF16)
    low = (x - high.astype(F32)).astype(BF16)
    return jnp.concatenate([high, low], axis=0)


def blend(frag, rank, limits, send, first, owners, capacity):
    pixel = iota((owners, frag.shape[-1]), 1).astype(F32)
    for slot in range(capacity):
        ranks = [rank[pl.ds((first * capacity + slot) * 4 + l, owners, stride=capacity * 4), :] for l in range(4)]
        value = [
            [
                frag[pl.ds((first * capacity + slot) * 16 + l * 4 + e, owners, stride=capacity * 16), :]
                for e in range(4)
            ]
            for l in range(4)
        ]
        clear = [1.0 - value[l][3] for l in range(4)]
        through = [None] * 4
        for l in range(4):
            for m in range(l):
                front = ranks[m] < ranks[l]
                behind = jnp.where(front, clear[m], 1.0)
                ahead = jnp.where(front, 1.0, clear[l])
                through[l] = behind if through[l] is None else through[l] * behind
                through[m] = ahead if through[m] is None else through[m] * ahead
        visible = pixel < limits[slot]
        for e in range(4):
            total = value[0][e] * through[0]
            for l in range(1, 4):
                total = total + value[l][e] * through[l]
            rows = pl.ds((first * capacity + slot) * 4 + e, owners, stride=capacity * 4)
            send[rows, :] = jnp.where(visible, total, 0.0)


def describe(slots, runs, order, place, blocks, owners, capacity, meta):
    width = meta.shape[1]
    lane = iota((owners, width), 1) & (blocks - 1)
    own = (lane >> log2(owners * capacity)) == place
    brick = (lane >> log2(capacity)) & (owners - 1)
    slot = lane & (capacity - 1)
    chosen = own & (brick == iota((owners, width), 0))
    live = slot.astype(F32) < column(slots.astype(F32), owners)
    runs = runs.astype(F32)
    run = jnp.broadcast_to(column(runs[0:1, :], owners), (owners, width))
    for c in range(1, capacity):
        run = jnp.where(slot == c, column(runs[c : c + 1, :], owners), run)
    key = jnp.sum(jnp.where(chosen & live, run + 1.0, 0.0), axis=0, keepdims=True)
    depth = column(order.astype(F32), owners) + (place * owners).astype(F32)
    rank = jnp.sum(jnp.where(chosen, depth, 0.0), axis=0, keepdims=True)
    row = iota(meta.shape, 0)
    meta[...] = jnp.where(row == 0, key, jnp.where(row == 1, rank, 0.0))


def exchange(sizes, frag_hbm, rank_hbm, count_hbm, slots_hbm, runs_hbm, order_hbm, lace_hbm,
             recv, earlier, target,
             frag, rank, count, slots, runs, order, lace, send, meta,
             load_sem, send_sem, recv_sem, meta_send, meta_recv):
    depths, tiles, bricks, owners, capacity, share = sizes
    d, t, b = lax.axis_index("depth"), lax.axis_index("tile"), lax.axis_index("brick")
    blocks = depths * owners * capacity
    group = capacity * 4

    half = tiles // 2
    part = half * bricks
    side = t // half
    firsts = [(1 - side) * part, side * part]

    def piece(src, dst, rows, h, sem):
        start = pl.multiple_of(firsts[h] * rows, part * rows)
        return pltpu.make_async_copy(
            src.at[pl.ds(start, part * rows)], dst.at[pl.ds(h * part * rows, part * rows)], sem
        )

    large = [
        [
            piece(frag_hbm, frag, capacity * 16, h, load_sem.at[2 * h]),
            piece(rank_hbm, rank, capacity * 4, h, load_sem.at[2 * h + 1]),
        ]
        for h in range(2)
    ]
    counts = pltpu.make_async_copy(count_hbm, count, load_sem.at[4])
    small = [
        pltpu.make_async_copy(src, dst, load_sem.at[5 + i])
        for i, (src, dst) in enumerate([
            (slots_hbm, slots), (runs_hbm, runs), (order_hbm, order), (lace_hbm, lace),
        ])
    ]
    for load in large[0] + large[1] + small[:3] + [counts] + small[3:]:
        load.start()

    def away(own, k):
        for bit in range(k.bit_length()):
            if k >> bit & 1:
                own = own + (1 - 2 * ((own // (1 << bit)) % 2)) * (1 << bit)
        return own

    mates = [[], []]
    for kt in list(range(half, tiles)) + list(range(half - 1, -1, -1)):
        for kb in range(bricks):
            for kd in range(depths):
                if kt or kb or kd:
                    mates[kt < half].append((away(d, kd), away(t, kt), away(b, kb)))
    partners = [(away(d, kd), t, b) for kd in range(1, depths)]
    others = len(mates[0]) + len(mates[1])
    barrier = pltpu.get_barrier_semaphore()
    for to in mates[0] + mates[1]:
        pl.semaphore_signal(barrier, inc=1, device_id=to, device_id_type=MESH)

    mine = t * bricks + b
    source = pl.ds(pl.multiple_of((d * owners + mine) * group, group), group)

    def outgoing(h, tile, brick):
        at = h * part + (tile % half) * bricks + brick
        return pl.ds(pl.multiple_of(at * group, group), group)

    for load in small[:3] + [counts]:
        load.wait()
    describe(slots[...], runs[...], order[...], d, blocks, owners, capacity, meta.at[d])
    limit = count[...].astype(F32)
    for h in range(2):
        limits = [column(limit[c : c + 1, :], part, firsts[h]) for c in range(capacity)]
        for load in large[h]:
            load.wait()
        blend(frag, rank, limits, send, h * part, part, capacity)

    pl.semaphore_wait(barrier, others)
    for to in partners:
        pltpu.make_async_remote_copy(
            src_ref=meta.at[d], dst_ref=meta.at[d], send_sem=meta_send, recv_sem=meta_recv,
            device_id=to, device_id_type=MESH,
        ).start()
    turns = [(i, h, to) for h in range(2) for i, to in enumerate(mates[h])]
    for _, h, to in sorted(turns, key=lambda turn: turn[:2]):
        pltpu.make_async_remote_copy(
            src_ref=send.at[outgoing(h, to[1], to[2])],
            dst_ref=recv.at[source], send_sem=send_sem, recv_sem=recv_sem,
            device_id=to, device_id_type=MESH,
        ).start()
    small[3].wait()
    recv[source, :] = send[outgoing(1, t, b), :]

    slots_total = lace.shape[0] * lace.shape[1]
    place = lace[...] - d * share
    shown = jnp.concatenate(
        [
            jnp.where(place[i : i + 1, :] == iota((share, lace.shape[1]), 0), 1.0, 0.0)
            for i in range(lace.shape[0])
        ],
        axis=1,
    ).astype(BF16)

    if partners:
        told = meta.at[pl.ds(0, depths - 1)]
        pltpu.make_async_copy(told, told, meta_recv).wait()
    known = meta[0]
    for s in range(1, depths):
        known = known + meta[s]
    key, rank_row = known[0:1, :], known[1:2, :]
    same = column(key, blocks) == key
    before = rank_row < column(rank_row, blocks)
    earlier[...] = jnp.where(same & before, 1.0, 0.0).astype(BF16)
    holds = iota((slots_total, 2 * blocks), 0).astype(F32) + 1.0 == key
    target[...] = jnp.dot(
        shown, jnp.where(holds, 1.0, 0.0).astype(BF16), preferred_element_type=F32
    ).astype(BF16)

    whole = recv.at[pl.ds(0, others * group)]
    pltpu.make_async_copy(whole, whole, recv_sem).wait()
    pltpu.make_async_copy(whole, whole, send_sem).wait()
    if partners:
        pltpu.make_async_copy(told, told, meta_send).wait()


def compose(recv, earlier, target, out, image, sem):
    blocks = earlier.shape[0]
    share = target.shape[0]
    clear = jnp.log(1.0 - recv[pl.ds(3, blocks, stride=4), :])
    passed = jnp.exp(jnp.dot(earlier[...], split(clear), preferred_element_type=F32))
    shaded = jnp.concatenate(
        [split(recv[pl.ds(e, blocks, stride=4), :] * passed) for e in range(4)], axis=1
    )
    width = recv.shape[1]
    pieces = sem.shape[0]
    rows = share // pieces
    writes = []
    for i in range(pieces):
        part = jnp.dot(
            target[i * rows : (i + 1) * rows, :], shaded, preferred_element_type=F32
        )
        for e in range(4):
            image[pl.ds(i * rows * 4 + e, rows, stride=4), :] = part[:, e * width : (e + 1) * width]
        where = pl.ds(i * rows * 4, rows * 4)
        writes.append(pltpu.make_async_copy(image.at[where], out.at[where], sem.at[i]))
        writes[-1].start()
    for write in writes:
        write.wait()


def shards(fragments, layer_rank, pixel_count, slot_count, block_run, brick_order, interlace):
    owners, capacity, width = fragments.shape[2], fragments.shape[3], fragments.shape[-1]
    runs_total = interlace.shape[0]
    depths, tiles, bricks = (lax.axis_size(a) for a in ("depth", "tile", "brick"))
    share = runs_total // depths
    blocks = depths * owners * capacity
    lanes = min(128, runs_total)
    args = [
        fragments.reshape(owners * capacity * 16, width),
        layer_rank.reshape(owners * capacity * 4, width),
        pixel_count.reshape(owners, capacity).T,
        slot_count.reshape(1, owners),
        block_run.reshape(owners, capacity).T,
        brick_order.reshape(1, owners),
        interlace.reshape(runs_total // lanes, lanes),
    ]
    vmem = pl.BlockSpec(memory_space=pltpu.VMEM)
    recv, earlier, target = pl.pallas_call(
        functools.partial(exchange, (depths, tiles, bricks, owners, capacity, share)),
        out_shape=(
            jax.ShapeDtypeStruct((blocks * 4, width), F32),
            jax.ShapeDtypeStruct((blocks, 2 * blocks), BF16),
            jax.ShapeDtypeStruct((share, 2 * blocks), BF16),
        ),
        in_specs=[pl.BlockSpec(memory_space=pltpu.HBM)] * len(args),
        out_specs=(vmem, vmem, vmem),
        scratch_shapes=[pltpu.VMEM(a.shape, a.dtype) for a in args]
        + [
            pltpu.VMEM((owners * capacity * 4, width), F32),
            pltpu.VMEM((depths, 8, 2 * blocks), F32),
            pltpu.SemaphoreType.DMA((len(args) + 2,)),
            pltpu.SemaphoreType.DMA,
            pltpu.SemaphoreType.DMA,
            pltpu.SemaphoreType.DMA,
            pltpu.SemaphoreType.DMA,
        ],
        compiler_params=pltpu.CompilerParams(
            collective_id=0, has_side_effects=True, vmem_limit_bytes=32 * 1024 * 1024
        ),
        name="exchange",
    )(*[pltpu.with_memory_space_constraint(a, pltpu.HBM) for a in args])
    image = pl.pallas_call(
        compose,
        out_shape=jax.ShapeDtypeStruct((share * 4, width), F32),
        in_specs=[vmem] * 3,
        out_specs=pl.BlockSpec(memory_space=pl.ANY),
        scratch_shapes=[
            pltpu.VMEM((share * 4, width), F32),
            pltpu.SemaphoreType.DMA((max(1, share // 32),)),
        ],
        compiler_params=pltpu.CompilerParams(vmem_limit_bytes=32 * 1024 * 1024),
        name="compose",
    )(recv, earlier, target)
    return image.reshape(1, 1, share, 4, width)


def solution(mesh):
    return jax.shard_map(
        shards,
        mesh=mesh,
        in_specs=(
            P("depth", ("tile", "brick"), None, None, None, None),
            P("depth", ("tile", "brick"), None, None, None, None),
            P("depth", ("tile", "brick"), None, None),
            P("depth", ("tile", "brick"), None),
            P("depth", ("tile", "brick"), None, None),
            P("depth", None),
            P(),
        ),
        out_specs=P(("tile", "brick"), "depth", None, None, None),
        check_vma=False,
    )
```
